32 devices in a mesh: grp: 2 (over y), seq: 16 (over z, x, core).
Axes of the slice: x: 2, y: 2, z: 4, core: 2. Of those that a mesh axis runs over, the one named last changes fastest.
Arguments:
- queries: bfloat16 [192, 8, 4096], P('seq', 'grp'), parts along dimension 1, may hold values from -7 to 7
- keys: bfloat16 [192, 8, 4096], P('seq', 'grp'), parts along dimension 1, may hold values from -7 to 7
- values: bfloat16 [192, 8, 4096], P('seq', 'grp'), parts along dimension 1, may hold values from -6 to 6
- clip_frames: int32 [8], P('grp'), parts along dimension 0, may hold values from 1 to 8, as said below
Outputs:
- attended: bfloat16 [192, 8, 4096], P('seq', 'grp'), parts along dimension 1
The draws below stay inside these ranges and needn't reach their ends.
There are 2 independent parts, one for each index of `grp`. The reference program is written for one: setup_inputs(seed, part) draws one part's arguments, and reference() takes and returns one part's arrays. A program takes and returns all parts, laid end to end along the dimension named above; each array names one. Nothing has to cross between parts.
Inputs may be any that keep to these rules, and one draw needn't show every extreme that they name: Tokens of clip s at positions clip_frames[s] * 24 and later hold no data; some clip has all 8 frames.
All inputs are finite; a program needn't handle non-finite values.
Results may differ from the reference program's by a relative error of at most 0.0048.
Values may be sent and summed in bfloat16 or wider, within the bound.
No kernel may reach another device: no remote copies, remote signals or barrier semaphores. Data moves between devices by JAX's collectives and lax.ppermute only.
A program may use at most 64 MiB of HBM per device.

```python
import math
import jax
import jax.numpy as jnp
from jax import lax

SEQS = 4
LENGTH = 192
HEADS = 32
HDIM = 128
HD = 4096
FRAMES = 8


def paired_fields(key):
    base_key = jax.random.fold_in(key, 17)
    query_key, key_key = jax.random.split(base_key, 2)
    field_shape = (LENGTH, SEQS, HEADS, HDIM)
    query_field = jnp.clip(1.8 * jax.random.normal(query_key, field_shape, jnp.float32), -7.0, 7.0)
    key_field = jnp.clip(1.8 * jax.random.normal(key_key, field_shape, jnp.float32), -7.0, 7.0)
    query_field = query_field.reshape(LENGTH, SEQS, HEADS * HDIM)
    key_field = key_field.reshape(LENGTH, SEQS, HEADS * HDIM)
    return (query_field, key_field)


def draw_queries(key, part):
    return paired_fields(key)[0].astype(jnp.bfloat16)


def draw_keys(key, part):
    return paired_fields(key)[1].astype(jnp.bfloat16)


def draw_clip_frames(key, part):
    base_key = jax.random.fold_in(key, 29)
    count_key, full_key = jax.random.split(base_key, 2)
    counts = jax.random.randint(count_key, (SEQS,), 1, FRAMES + 1)
    full_clip = jax.random.randint(full_key, (), 0, SEQS)
    return counts.at[full_clip].set(FRAMES).astype(jnp.int32)


def steps_of(key, shape, pieces, low, top_value):
    def one(dim, blocks):
        draws = jax.random.uniform(jax.random.fold_in(jax.random.fold_in(key, 6), dim), (blocks,), jnp.float32, low / len(pieces), top_value / len(pieces))
        return jnp.repeat(jnp.exp(draws), shape[dim] // blocks).reshape((-1,) + (1,) * (len(shape) - dim - 1))

    loudness = one(*pieces[0])
    for cut in pieces[1:]:
        loudness = loudness * one(*cut)
    return loudness


def scatter_about(stream_key, shape, deviation, limit, shards=(), kind=jnp.bfloat16):
    array = jax.random.normal(stream_key, shape, jnp.float32) * deviation
    if len(shards) > 0:
        array = steps_of(stream_key, shape, shards, -0.22, 0.18) * array
    return jnp.clip(array, min=-limit, max=limit).astype(kind)


def setup_inputs(seed: int = 0, part: int = 0) -> dict:
    streams_of = jax.random.split(jax.random.key(seed), 5)
    own_keys = jax.random.split(jax.random.fold_in(streams_of[4], part), 5)
    return {
        "queries": draw_queries(jax.random.fold_in(jax.random.fold_in(streams_of[4], part), 71), part),
        "keys": draw_keys(jax.random.fold_in(jax.random.fold_in(streams_of[4], part), 71), part),
        "values": scatter_about(own_keys[2], (LENGTH, SEQS, HD), 1.0, 6.0, ((0, 16),)),
        "clip_frames": draw_clip_frames(jax.random.fold_in(jax.random.fold_in(streams_of[4], part), 71), part),
    }


def reference(queries, keys, values, clip_frames):
    item_count = SEQS * HEADS
    score_scale = 1.0 / math.sqrt(HDIM)
    query_items = jnp.transpose(queries.reshape(LENGTH, item_count, HDIM), (1, 0, 2))
    key_items = jnp.transpose(keys.reshape(LENGTH, item_count, HDIM), (1, 0, 2))
    value_items = jnp.transpose(values.reshape(LENGTH, item_count, HDIM), (1, 0, 2))
    limits = jnp.repeat(clip_frames * (LENGTH // FRAMES), HEADS)
    positions = jnp.arange(LENGTH, dtype=jnp.int32)

    def attend_item(operands):
        query_rows, key_rows, value_rows, limit_value = operands
        scores = jnp.dot(query_rows, key_rows.T, preferred_element_type=jnp.float32) * score_scale
        scores = jnp.where(positions[None, :] < limit_value, scores, -jnp.inf)
        row_max = lax.optimization_barrier(jnp.max(scores, axis=1, keepdims=True))
        exponent = jnp.exp(scores - row_max)
        weights = (exponent / lax.optimization_barrier(jnp.sum(exponent, axis=1, keepdims=True))).astype(jnp.bfloat16)
        return jnp.dot(weights, value_rows, preferred_element_type=jnp.float32).astype(jnp.bfloat16)
    outputs = lax.map(attend_item, (query_items, key_items, value_items, limits))
    return jnp.transpose(outputs, (1, 0, 2)).reshape(LENGTH, SEQS, HEADS * HDIM)
```

```python
import math
import jax
import jax.numpy as jnp
from jax import lax
from jax.sharding import PartitionSpec as P

HEADS = 32
HDIM = 128
FRAMES = 8
neg_large = -1e30

def attend(query_rows, key_rows, value_rows, key_bias):
    scores = jnp.einsum("qnd,knd->nqk", query_rows, key_rows, preferred_element_type=jnp.float32)
    scores = scores * (1.0 / math.sqrt(HDIM)) + key_bias[:, None, :]
    row_max = jnp.max(scores, axis=2, keepdims=True)
    exponent = jnp.exp(scores - row_max)
    weights = (exponent / jnp.sum(exponent, axis=2, keepdims=True)).astype(jnp.bfloat16)
    combined = jnp.einsum("nqk,knd->qnd", weights, value_rows, preferred_element_type=jnp.float32)
    return combined.astype(jnp.bfloat16)

def body(queries, keys, values, clip_frames):
    tokens, seq_count, feature_dim = queries.shape
    devices = lax.axis_size("seq")
    me = lax.axis_index("seq")
    slot_count = seq_count * HEADS
    per_device = slot_count // devices
    length = tokens * devices
    frame_tokens = length // FRAMES
    own = (jnp.arange(per_device, dtype=jnp.int32) + me * per_device) // HEADS
    limit = clip_frames[own] * frame_tokens
    place = jnp.arange(length, dtype=jnp.int32)
    key_bias = jnp.where(place[None, :] < limit[:, None], 0.0, neg_large).astype(jnp.float32)
    packed = jnp.stack([x.reshape(tokens, devices, per_device, HDIM) for x in (queries, keys, values)])
    packed = jnp.transpose(packed, (2, 0, 1, 3, 4))
    got = lax.all_to_all(packed, "seq", split_axis=0, concat_axis=0, tiled=True)
    got = jnp.transpose(got, (1, 0, 2, 3, 4)).reshape(3, length, per_device, HDIM)
    combined = attend(got[0], got[1], got[2], key_bias)
    combined = combined.reshape(devices, tokens, per_device, HDIM)
    returned = lax.all_to_all(combined, "seq", split_axis=0, concat_axis=0, tiled=True)
    return jnp.transpose(returned, (1, 0, 2, 3)).reshape(tokens, seq_count, feature_dim)

def solution(mesh):
    return jax.shard_map(
        body, mesh=mesh,
        in_specs=(P("seq", "grp", None), P("seq", "grp", None), P("seq", "grp", None), P("grp")),
        out_specs=P("seq", "grp", None), check_vma=False)
```

```python
import functools
import math
import jax
import jax.numpy as jnp
from jax import lax
from jax.experimental import pallas as pl
from jax.experimental.pallas import tpu as pltpu
from jax.sharding import PartitionSpec as P

HEADS = 32
HDIM = 128
FRAMES = 8
neg_large = -1e30
VM = pl.BlockSpec(memory_space=pltpu.VMEM)
HB = pl.BlockSpec(memory_space=pltpu.HBM)
SM = pl.BlockSpec(memory_space=pltpu.SMEM)
LARGE = pltpu.CompilerParams(vmem_limit_bytes=24 * 1024 * 1024)
SMALL = pltpu.CompilerParams(vmem_limit_bytes=8 * 1024 * 1024)


def cost(micros):
    return pl.CostEstimate(flops=int(micros * 1e9), bytes_accessed=int(micros * 3e6), transcendentals=0)


def position(outer):
    me = lax.axis_index("seq")
    return me // (lax.axis_size("seq") // outer), me % 2


def pack_kernel(outer, *refs):
    srcs, (own, peer, sem) = refs[:-3], refs[-3:]
    heads = own.shape[3]
    line, core = position(outer)
    copies = []
    for i, dst in ((1, peer), (0, own)):
        for a in range(outer):
            group = jnp.bitwise_xor(line, a) * 2 + jnp.bitwise_xor(core, i)
            for j, src in enumerate(srcs):
                copies.append(pltpu.make_async_copy(
                    src.at[:, pl.ds(group * heads, heads)], dst.at[a, j], sem.at[i, a, j]))
    for c in copies:
        c.start()
    for c in copies:
        c.wait()


def pack(outer, *srcs):
    tokens, _, clips, _ = srcs[0].shape
    heads = HEADS // (2 * outer)
    shape = jax.ShapeDtypeStruct((outer, len(srcs), tokens, heads, clips, HDIM), jnp.bfloat16)
    own, peer = pl.pallas_call(
        functools.partial(pack_kernel, outer),
        out_shape=[shape, shape], in_specs=[HB] * len(srcs), out_specs=[VM, VM],
        scratch_shapes=[pltpu.SemaphoreType.DMA((2, outer, len(srcs)))], compiler_params=SMALL,
    )(*srcs)
    shape = (outer, len(srcs), tokens, heads * clips, HDIM)
    return own.reshape(shape), peer.reshape(shape)


def turn(pieces, j):
    return jnp.swapaxes(jnp.concatenate([x[j, c] for x in pieces for c in range(2)], axis=0), 0, 1)


def query_kernel(*refs):
    srcs, out = refs[:-1], refs[-1]
    out[...] = turn(srcs, 0)


def near_kernel(marks, frame_tokens, frames_ref, *refs):
    kvs, (k_out, v_out, bias_out) = refs[:-3], refs[-3:]
    k_out[...] = turn(kvs, 0)
    v_out[...] = turn(kvs, 1)
    clips, length = bias_out.shape
    tokens = length // len(marks)
    me = lax.axis_index("seq")
    key = lax.broadcasted_iota(jnp.int32, (1, length), 1)
    place = jnp.zeros((1, length), jnp.int32)
    for s, mark in enumerate(marks):
        start = jnp.bitwise_xor(me, mark) * tokens - s * tokens
        place = jnp.where(key >= s * tokens, key + start, place)
    for c in range(clips):
        bias_out[c:c + 1, :] = jnp.where(place < frames_ref[c] * frame_tokens, 0.0, neg_large)


def main_kernel(nkv, q, *refs):
    kvs, (k_near, v_near, bias), outs = refs[:nkv], refs[nkv:nkv + 3], refs[nkv + 3:]
    k = jnp.concatenate([k_near[...], turn(kvs, 0)], axis=1)
    v = jnp.concatenate([v_near[...], turn(kvs, 1)], axis=1)
    slots = k.shape[0]
    clips = bias.shape[0]
    s = lax.dot_general(q[...], k, (((2,), (2,)), ((0,), (0,))), preferred_element_type=jnp.float32)
    s = s * (1.0 / math.sqrt(HDIM)) + jnp.concatenate([bias[...]] * (slots // clips), axis=0)[:, None, :]
    e = jnp.exp(s - jnp.max(s, axis=2, keepdims=True))
    w = (e / jnp.sum(e, axis=2, keepdims=True)).astype(jnp.bfloat16)
    o = lax.dot_general(w, v, (((2,), (1,)), ((0,), (0,))), preferred_element_type=jnp.float32)
    o = jnp.swapaxes(o.astype(jnp.bfloat16), 0, 1)
    tokens = outs[0].shape[1]
    for i, out in enumerate(outs):
        for c in range(2):
            out[c] = o[(2 * i + c) * tokens:(2 * i + c + 1) * tokens]


def unpack_kernel(outer, order, *refs):
    kept, came, out = refs[:outer], refs[outer:-1], refs[-1]
    heads = kept[0].shape[2]
    line, core = position(outer)
    for i, a in enumerate(order):
        group = jnp.bitwise_xor(line, a) * 2
        out[:, pl.ds((group + core) * heads, heads)] = kept[i][0]
        out[:, pl.ds((group + 1 - core) * heads, heads)] = came[i][1]


def after(x, y):
    y = y[(0,) * (y.ndim - 1)]
    return jnp.where(y == y, x, jnp.zeros_like(x))


def body(queries, keys, values, clip_frames):
    tokens, clips, features = queries.shape
    devices = lax.axis_size("seq")
    outer = 1
    while outer * outer < devices:
        outer *= 2
    inner = devices // outer
    heads = HEADS // (2 * outer)
    slots = heads * clips
    length = tokens * devices
    bf = jnp.bfloat16

    def swap(x, mask):
        return lax.ppermute(x, "seq", [(i, i ^ mask) for i in range(devices)])

    far = list(range(outer - 1, outer // 2 - 1, -1))
    near = list(range(outer // 2 - 1, -1, -1))
    srcs = [jnp.transpose(x.reshape(tokens, clips, HEADS, HDIM), (0, 2, 1, 3)) for x in (keys, values, queries)]
    kv_own, kv_peer = pack(outer, *srcs[:2])
    q_own, q_peer = pack(outer, srcs[2])
    kv_got, q_got = swap(kv_peer, 1), swap(q_peer, 1)
    kv, qs = {}, {}
    for a in far + near:
        pay = jnp.stack([kv_own[a], kv_got[a]], axis=1)
        kv[a] = swap(pay, a * inner) if a else pay
    for a in far + near:
        pay = jnp.stack([q_own[a], q_got[a]], axis=1)
        if 1 and a:
            pay = after(pay, kv[near[0]])
        qs[a] = swap(pay, a * inner) if a else pay

    def plane(part):
        pieces, marks = [], []
        for a in part:
            stack, mark = [kv[a]], [a * inner]
            step = inner // 2
            while step > 1:
                stack = stack + [swap(x[:2], step) for x in stack]
                mark = mark + [m ^ step for m in mark]
                step //= 2
            pieces += stack
            marks += [m ^ c for m in mark for c in (0, 1)]
        return pieces, marks

    near_pieces, near_marks = plane(near[::-1])
    far_pieces, far_marks = plane(far)
    marks = near_marks + far_marks
    some = jax.ShapeDtypeStruct((slots, length // 2, HDIM), bf)
    k_near, v_near, bias = pl.pallas_call(
        functools.partial(near_kernel, marks, length // FRAMES),
        out_shape=[some, some, jax.ShapeDtypeStruct((clips, length), jnp.float32)],
        in_specs=[SM] + [VM] * len(near_pieces), out_specs=[VM] * 3,
        compiler_params=LARGE, cost_estimate=cost(0.01),
    )(clip_frames, *near_pieces)
    parts = far + near
    q = pl.pallas_call(
        query_kernel, out_shape=jax.ShapeDtypeStruct((slots, outer * 2 * tokens, HDIM), bf),
        in_specs=[VM] * outer, out_specs=VM, compiler_params=SMALL, cost_estimate=cost(0.01),
    )(*[qs[a] for a in parts])
    piece = jax.ShapeDtypeStruct((2, tokens, slots, HDIM), bf)
    res = pl.pallas_call(
        functools.partial(main_kernel, len(far_pieces)),
        out_shape=[piece] * outer,
        in_specs=[VM] * (len(far_pieces) + 4), out_specs=[VM] * outer,
        compiler_params=LARGE, cost_estimate=cost(2),
    )(q, *far_pieces, k_near, v_near, bias)
    outs = [swap(o, a * inner) if a else o for a, o in zip(parts, res)]
    came = [swap(o, 1) for o in outs]
    out = pl.pallas_call(
        functools.partial(unpack_kernel, outer, parts),
        out_shape=jax.ShapeDtypeStruct((tokens, HEADS, clips, HDIM), bf),
        in_specs=[VM] * (2 * outer), out_specs=VM, compiler_params=SMALL,
    )(*[x.reshape(2, tokens, heads, clips, HDIM) for x in outs + came])
    return jnp.transpose(out, (0, 2, 1, 3)).reshape(tokens, clips, features)


def solution(mesh):
    return jax.shard_map(
        body, mesh=mesh,
        in_specs=(P("seq", "grp", None), P("seq", "grp", None), P("seq", "grp", None), P("grp")),
        out_specs=P("seq", "grp", None), check_vma=False)
```

```python
import functools
import math
import jax
import jax.numpy as jnp
from jax import lax
from jax.experimental import pallas as pl
from jax.experimental.pallas import tpu as pltpu
from jax.sharding import PartitionSpec as P

HEADS = 32
HDIM = 128
FRAMES = 8
neg_large = -1e30
VM = pl.BlockSpec(memory_space=pltpu.VMEM)
HB = pl.BlockSpec(memory_space=pltpu.HBM)
SM = pl.BlockSpec(memory_space=pltpu.SMEM)
LARGE = pltpu.CompilerParams(vmem_limit_bytes=24 * 1024 * 1024)
SMALL = pltpu.CompilerParams(vmem_limit_bytes=8 * 1024 * 1024)


def cost(micros):
    return pl.CostEstimate(flops=int(micros * 1e9), bytes_accessed=int(micros * 3e6), transcendentals=0)


def position(outer):
    me = lax.axis_index("seq")
    return me // (lax.axis_size("seq") // outer), me % 2


def pack_kernel(outer, *refs):
    srcs, (own, peer, sem) = refs[:-3], refs[-3:]
    heads = own.shape[3]
    line, core = position(outer)
    copies = []
    for i, dst in ((1, peer), (0, own)):
        for a in range(outer):
            group = jnp.bitwise_xor(line, a) * 2 + jnp.bitwise_xor(core, i)
            for j, src in enumerate(srcs):
                copies.append(pltpu.make_async_copy(
                    src.at[:, pl.ds(group * heads, heads)], dst.at[a, j], sem.at[i, a, j]))
    for c in copies:
        c.start()
    for c in copies:
        c.wait()


def pack(outer, *srcs):
    tokens, _, clips, _ = srcs[0].shape
    heads = HEADS // (2 * outer)
    shape = jax.ShapeDtypeStruct((outer, len(srcs), tokens, heads, clips, HDIM), jnp.bfloat16)
    own, peer = pl.pallas_call(
        functools.partial(pack_kernel, outer),
        out_shape=[shape, shape], in_specs=[HB] * len(srcs), out_specs=[VM, VM],
        scratch_shapes=[pltpu.SemaphoreType.DMA((2, outer, len(srcs)))], compiler_params=SMALL,
    )(*srcs)
    shape = (outer, len(srcs), tokens, heads * clips, HDIM)
    return own.reshape(shape), peer.reshape(shape)


def turn(pieces, j):
    return jnp.swapaxes(jnp.concatenate([x[j, c] for x in pieces for c in range(2)], axis=0), 0, 1)


def query_kernel(*refs):
    srcs, out = refs[:-1], refs[-1]
    out[...] = turn(srcs, 0)


def near_kernel(marks, frame_tokens, frames_ref, *refs):
    kvs, (k_out, v_out, bias_out) = refs[:-3], refs[-3:]
    k_out[...] = turn(kvs, 0)
    v_out[...] = turn(kvs, 1)
    clips, length = bias_out.shape
    tokens = length // len(marks)
    me = lax.axis_index("seq")
    key = lax.broadcasted_iota(jnp.int32, (1, length), 1)
    place = jnp.zeros((1, length), jnp.int32)
    for s, mark in enumerate(marks):
        start = jnp.bitwise_xor(me, mark) * tokens - s * tokens
        place = jnp.where(key >= s * tokens, key + start, place)
    for c in range(clips):
        bias_out[c:c + 1, :] = jnp.where(place < frames_ref[c] * frame_tokens, 0.0, neg_large)


def main_kernel(nkv, q, *refs):
    kvs, (k_near, v_near, bias), outs = refs[:nkv], refs[nkv:nkv + 3], refs[nkv + 3:]
    k = jnp.concatenate([k_near[...], turn(kvs, 0)], axis=1)
    v = jnp.concatenate([v_near[...], turn(kvs, 1)], axis=1)
    slots = k.shape[0]
    clips = bias.shape[0]
    s = lax.dot_general(q[...], k, (((2,), (2,)), ((0,), (0,))), preferred_element_type=jnp.float32)
    s = s * (1.0 / math.sqrt(HDIM)) + jnp.concatenate([bias[...]] * (slots // clips), axis=0)[:, None, :]
    e = jnp.exp(s - jnp.max(s, axis=2, keepdims=True))
    w = (e / jnp.sum(e, axis=2, keepdims=True)).astype(jnp.bfloat16)
    o = lax.dot_general(w, v, (((2,), (1,)), ((0,), (0,))), preferred_element_type=jnp.float32)
    o = jnp.swapaxes(o.astype(jnp.bfloat16), 0, 1)
    tokens = outs[0].shape[1]
    for i, out in enumerate(outs):
        for c in range(2):
            out[c] = o[(2 * i + c) * tokens:(2 * i + c + 1) * tokens]


def unpack_kernel(outer, order, *refs):
    kept, came, out = refs[:outer], refs[outer:-1], refs[-1]
    heads = kept[0].shape[2]
    line, core = position(outer)
    for i, a in enumerate(order):
        group = jnp.bitwise_xor(line, a) * 2
        out[:, pl.ds((group + core) * heads, heads)] = kept[i][0]
        out[:, pl.ds((group + 1 - core) * heads, heads)] = came[i][1]


def after(x, y):
    y = y[(0,) * (y.ndim - 1)]
    return jnp.where(y == y, x, jnp.zeros_like(x))


def body(queries, keys, values, clip_frames):
    tokens, clips, features = queries.shape
    devices = lax.axis_size("seq")
    outer = 1
    while outer * outer < devices:
        outer *= 2
    inner = devices // outer
    heads = HEADS // (2 * outer)
    slots = heads * clips
    length = tokens * devices
    bf = jnp.bfloat16

    def swap(x, mask):
        return lax.ppermute(x, "seq", [(i, i ^ mask) for i in range(devices)])

    far = list(range(outer - 1, outer // 2 - 1, -1))
    near = list(range(outer // 2 - 1, -1, -1))
    srcs = [jnp.transpose(x.reshape(tokens, clips, HEADS, HDIM), (0, 2, 1, 3)) for x in (keys, values, queries)]
    kv_own, kv_peer = pack(outer, *srcs[:2])
    q_own, q_peer = pack(outer, srcs[2])
    kv_got, q_got = swap(kv_peer, 1), swap(q_peer, 1)
    late = far[len(far) // 2:]
    kv, qs = {}, {}
    for a in far + near:
        pay = jnp.stack([kv_own[a], kv_got[a]], axis=1)
        kv[a] = swap(pay, a * inner) if a else pay
    def plane(part):
        pieces = []
        for a in part:
            stack = [kv[a]]
            step = inner // 2
            while step > 1:
                stack = stack + [swap(x, step) for x in stack]
                step //= 2
            pieces += stack
        return pieces

    order = [0]
    step = inner // 2
    while step > 1:
        order = order + [m ^ step for m in order]
        step //= 2
    marks = [(a * inner) ^ m ^ c for a in near[::-1] + far for m in order for c in (0, 1)]
    near_pieces = plane(near[::-1])
    some = jax.ShapeDtypeStruct((slots, length // 2, HDIM), bf)
    k_near, v_near, bias = pl.pallas_call(
        functools.partial(near_kernel, marks, length // FRAMES),
        out_shape=[some, some, jax.ShapeDtypeStruct((clips, length), jnp.float32)],
        in_specs=[SM] + [VM] * len(near_pieces), out_specs=[VM] * 3,
        compiler_params=LARGE, cost_estimate=cost(.01),
    )(clip_frames, *near_pieces)
    for a in far + near:
        pay = jnp.stack([q_own[a], q_got[a]], axis=1)
        if a and (a in far and 3 & 1 or a in near and 3 & 2):
            pay = after(pay, k_near)
        if a and (a in far and 3 & 4 or a in near and 3 & 8):
            pay = after(pay, kv[near[0]])
        qs[a] = swap(pay, a * inner) if a else pay
    for a in late:
        if 1:
            kv[a] = after(kv[a], k_near)
    far_pieces = plane(far)
    parts = far + near
    q = pl.pallas_call(
        query_kernel, out_shape=jax.ShapeDtypeStruct((slots, outer * 2 * tokens, HDIM), bf),
        in_specs=[VM] * outer, out_specs=VM, compiler_params=SMALL, cost_estimate=cost(1.0),
    )(*[qs[a] for a in parts])
    piece = jax.ShapeDtypeStruct((2, tokens, slots, HDIM), bf)
    res = pl.pallas_call(
        functools.partial(main_kernel, len(far_pieces)),
        out_shape=[piece] * outer,
        in_specs=[VM] * (len(far_pieces) + 4), out_specs=[VM] * outer,
        compiler_params=LARGE, cost_estimate=cost(2),
    )(q, *far_pieces, k_near, v_near, bias)
    outs = [swap(o, a * inner) if a else o for a, o in zip(parts, res)]
    came = [swap(o, 1) for o in outs]
    out = pl.pallas_call(
        functools.partial(unpack_kernel, outer, parts),
        out_shape=jax.ShapeDtypeStruct((tokens, HEADS, clips, HDIM), bf),
        in_specs=[VM] * (2 * outer), out_specs=VM, compiler_params=SMALL,
    )(*[x.reshape(2, tokens, heads, clips, HDIM) for x in outs + came])
    return jnp.transpose(out, (0, 2, 1, 3)).reshape(tokens, clips, features)


def solution(mesh):
    return jax.shard_map(
        body, mesh=mesh,
        in_specs=(P("seq", "grp", None), P("seq", "grp", None), P("seq", "grp", None), P("grp")),
        out_specs=P("seq", "grp", None), check_vma=False)
```

```python
import functools
import math
import jax
import jax.numpy as jnp
from jax import lax
from jax.experimental import pallas as pl
from jax.experimental.pallas import tpu as pltpu
from jax.sharding import PartitionSpec as P

HEADS = 32
HDIM = 128
FRAMES = 8
neg_large = -1e30
VM = pl.BlockSpec(memory_space=pltpu.VMEM)
HB = pl.BlockSpec(memory_space=pltpu.HBM)
SM = pl.BlockSpec(memory_space=pltpu.SMEM)
LARGE = pltpu.CompilerParams(vmem_limit_bytes=24 * 1024 * 1024)
SMALL = pltpu.CompilerParams(vmem_limit_bytes=8 * 1024 * 1024)


def cost(micros):
    return pl.CostEstimate(flops=int(micros * 1e9), bytes_accessed=int(micros * 3e6), transcendentals=0)


def position(outer):
    me = lax.axis_index("seq")
    return me // (lax.axis_size("seq") // outer), me % 2


def pack_kernel(outer, *refs):
    srcs, (own, peer, sem) = refs[:-3], refs[-3:]
    heads = own.shape[3]
    line, core = position(outer)
    copies = []
    for i, dst in ((1, peer), (0, own)):
        for a in range(outer):
            group = jnp.bitwise_xor(line, a) * 2 + jnp.bitwise_xor(core, i)
            for j, src in enumerate(srcs):
                copies.append(pltpu.make_async_copy(
                    src.at[:, pl.ds(group * heads, heads)], dst.at[a, j], sem.at[i, a, j]))
    for c in copies:
        c.start()
    for c in copies:
        c.wait()


def pack(outer, *srcs):
    tokens, _, clips, _ = srcs[0].shape
    heads = HEADS // (2 * outer)
    shape = jax.ShapeDtypeStruct((outer, len(srcs), tokens, heads, clips, HDIM), jnp.bfloat16)
    own, peer = pl.pallas_call(
        functools.partial(pack_kernel, outer),
        out_shape=[shape, shape], in_specs=[HB] * len(srcs), out_specs=[VM, VM],
        scratch_shapes=[pltpu.SemaphoreType.DMA((2, outer, len(srcs)))], compiler_params=SMALL,
    )(*srcs)
    shape = (outer, len(srcs), tokens, heads * clips, HDIM)
    return own.reshape(shape), peer.reshape(shape)


def turn(pieces, j):
    return jnp.swapaxes(jnp.concatenate([x[j, c] for x in pieces for c in range(2)], axis=0), 0, 1)


def query_kernel(*refs):
    srcs, out = refs[:-1], refs[-1]
    out[...] = turn(srcs, 0)


def near_kernel(marks, frame_tokens, frames_ref, *refs):
    kvs, (k_out, v_out, bias_out) = refs[:-3], refs[-3:]
    k_out[...] = turn(kvs, 0)
    v_out[...] = turn(kvs, 1)
    clips, length = bias_out.shape
    tokens = length // len(marks)
    me = lax.axis_index("seq")
    key = lax.broadcasted_iota(jnp.int32, (1, length), 1)
    place = jnp.zeros((1, length), jnp.int32)
    for s, mark in enumerate(marks):
        start = jnp.bitwise_xor(me, mark) * tokens - s * tokens
        place = jnp.where(key >= s * tokens, key + start, place)
    for c in range(clips):
        bias_out[c:c + 1, :] = jnp.where(place < frames_ref[c] * frame_tokens, 0.0, neg_large)


def main_kernel(nkv, q, *refs):
    kvs, (k_near, v_near, bias), outs = refs[:nkv], refs[nkv:nkv + 3], refs[nkv + 3:]
    k = jnp.concatenate([k_near[...], turn(kvs, 0)], axis=1)
    v = jnp.concatenate([v_near[...], turn(kvs, 1)], axis=1)
    slots = k.shape[0]
    clips = bias.shape[0]
    s = lax.dot_general(q[...], k, (((2,), (2,)), ((0,), (0,))), preferred_element_type=jnp.float32)
    s = s * (1.0 / math.sqrt(HDIM)) + jnp.concatenate([bias[...]] * (slots // clips), axis=0)[:, None, :]
    e = jnp.exp(s - jnp.max(s, axis=2, keepdims=True))
    w = (e / jnp.sum(e, axis=2, keepdims=True)).astype(jnp.bfloat16)
    o = lax.dot_general(w, v, (((2,), (1,)), ((0,), (0,))), preferred_element_type=jnp.float32)
    o = jnp.swapaxes(o.astype(jnp.bfloat16), 0, 1)
    tokens = outs[0].shape[1]
    for i, out in enumerate(outs):
        for c in range(2):
            out[c] = o[(2 * i + c) * tokens:(2 * i + c + 1) * tokens]


def unpack_kernel(outer, order, *refs):
    kept, came, out = refs[:outer], refs[outer:-1], refs[-1]
    heads = kept[0].shape[2]
    line, core = position(outer)
    for i, a in enumerate(order):
        group = jnp.bitwise_xor(line, a) * 2
        out[:, pl.ds((group + core) * heads, heads)] = kept[i][0]
        out[:, pl.ds((group + 1 - core) * heads, heads)] = came[i][1]


def after(x, y):
    y = y[(0,) * (y.ndim - 1)]
    return jnp.where(y == y, x, jnp.zeros_like(x))


def body(queries, keys, values, clip_frames):
    tokens, clips, features = queries.shape
    devices = lax.axis_size("seq")
    outer = 1
    while outer * outer < devices:
        outer *= 2
    inner = devices // outer
    heads = HEADS // (2 * outer)
    slots = heads * clips
    length = tokens * devices
    bf = jnp.bfloat16

    def swap(x, mask):
        return lax.ppermute(x, "seq", [(i, i ^ mask) for i in range(devices)])

    far = list(range(outer - 1, outer // 2 - 1, -1))
    near = list(range(outer // 2 - 1, -1, -1))
    srcs = [jnp.transpose(x.reshape(tokens, clips, HEADS, HDIM), (0, 2, 1, 3)) for x in (keys, values, queries)]
    kv_own, kv_peer = pack(outer, *srcs[:2])
    q_own, q_peer = pack(outer, srcs[2])
    kv_got, q_got = swap(kv_peer, 1), swap(q_peer, 1)
    late = far[len(far) // 2:]
    kv, qs = {}, {}
    for a in far + near:
        pay = jnp.stack([kv_own[a], kv_got[a]], axis=1)
        kv[a] = swap(pay, a * inner) if a else pay
    def plane(part):
        pieces = []
        for a in part:
            stack = [kv[a]]
            step = inner // 2
            while step > 1:
                stack = stack + [swap(x, step) for x in stack]
                step //= 2
            pieces += stack
        return pieces

    order = [0]
    step = inner // 2
    while step > 1:
        order = order + [m ^ step for m in order]
        step //= 2
    marks = [(a * inner) ^ m ^ c for a in near[::-1] + far for m in order for c in (0, 1)]
    kv[0] = after(kv[0], kv[near[0]])
    near_pieces = plane(near[::-1])
    some = jax.ShapeDtypeStruct((slots, length // 2, HDIM), bf)
    k_near, v_near, bias = pl.pallas_call(
        functools.partial(near_kernel, marks, length // FRAMES),
        out_shape=[some, some, jax.ShapeDtypeStruct((clips, length), jnp.float32)],
        in_specs=[SM] + [VM] * len(near_pieces), out_specs=[VM] * 3,
        compiler_params=LARGE, cost_estimate=cost(.01),
    )(clip_frames, *near_pieces)
    for a in far + near:
        pay = jnp.stack([q_own[a], q_got[a]], axis=1)
        if a:
            pay = after(pay, k_near)
        qs[a] = swap(pay, a * inner) if a else pay
    for a in late:
        kv[a] = after(kv[a], k_near)
    far_pieces = plane(far)
    parts = far + near
    q = pl.pallas_call(
        query_kernel, out_shape=jax.ShapeDtypeStruct((slots, outer * 2 * tokens, HDIM), bf),
        in_specs=[VM] * outer, out_specs=VM, compiler_params=SMALL, cost_estimate=cost(1.0),
    )(*[qs[a] for a in parts])
    piece = jax.ShapeDtypeStruct((2, tokens, slots, HDIM), bf)
    res = pl.pallas_call(
        functools.partial(main_kernel, len(far_pieces)),
        out_shape=[piece] * outer,
        in_specs=[VM] * (len(far_pieces) + 4), out_specs=[VM] * outer,
        compiler_params=LARGE, cost_estimate=cost(2),
    )(q, *far_pieces, k_near, v_near, bias)
    outs = [swap(o, a * inner) if a else o for a, o in zip(parts, res)]
    came = [swap(o, 1) for o in outs]
    out = pl.pallas_call(
        functools.partial(unpack_kernel, outer, parts),
        out_shape=jax.ShapeDtypeStruct((tokens, HEADS, clips, HDIM), bf),
        in_specs=[VM] * (2 * outer), out_specs=VM, compiler_params=SMALL,
    )(*[x.reshape(2, tokens, heads, clips, HDIM) for x in outs + came])
    return jnp.transpose(out, (0, 2, 1, 3)).reshape(tokens, clips, features)


def solution(mesh):
    return jax.shard_map(
        body, mesh=mesh,
        in_specs=(P("seq", "grp", None), P("seq", "grp", None), P("seq", "grp", None), P("grp")),
        out_specs=P("seq", "grp", None), check_vma=False)
```

```python
import functools
import math

import jax
import jax.numpy as jnp
from jax import lax
from jax.experimental import pallas as pl
from jax.experimental.pallas import tpu as pltpu
from jax.sharding import PartitionSpec as P

HEADS = 32
HDIM = 128
FRAMES = 8
neg_large = -1e30
VM = pl.BlockSpec(memory_space=pltpu.VMEM)
ANY = pl.BlockSpec(memory_space=pl.ANY)
SM = pl.BlockSpec(memory_space=pltpu.SMEM)
LARGE = pltpu.CompilerParams(vmem_limit_bytes=24 * 1024 * 1024)
SMALL = pltpu.CompilerParams(vmem_limit_bytes=8 * 1024 * 1024)


def cost(micros):
    return pl.CostEstimate(flops=int(micros * 1e9), bytes_accessed=int(micros * 3e6), transcendentals=0)


def position(outer):
    me = lax.axis_index("seq")
    return me // (lax.axis_size("seq") // outer), me % 2


def pack_kernel(outer, count, *refs):
    srcs, dsts, sem = refs[:count], refs[count:-1], refs[-1]
    heads = dsts[0].shape[3]
    line, core = position(outer)
    copies = []
    for dst, flip in zip(dsts, (1, 0)):
        for a in range(outer):
            group = jnp.bitwise_xor(line, a) * 2 + jnp.bitwise_xor(core, flip)
            for j, src in enumerate(srcs):
                copies.append(pltpu.make_async_copy(
                    src.at[:, pl.ds(group * heads, heads)], dst.at[j, a], sem.at[len(copies)]))
    for c in copies:
        c.start()
    for c in copies:
        c.wait()


def pack(outer, *srcs):
    tokens, _, clips, _ = srcs[0].shape
    heads = HEADS // (2 * outer)
    shape = jax.ShapeDtypeStruct((len(srcs), outer, tokens, heads, clips, HDIM), jnp.bfloat16)
    out = pl.pallas_call(
        functools.partial(pack_kernel, outer, len(srcs)),
        out_shape=[shape, shape], in_specs=[ANY] * len(srcs), out_specs=[VM, VM],
        scratch_shapes=[pltpu.SemaphoreType.DMA((2 * outer * len(srcs),))], compiler_params=SMALL,
    )(*srcs)
    return [x.reshape(x.shape[:3] + (heads * clips, HDIM)) for x in out]


def turn(pieces, j):
    return jnp.swapaxes(jnp.concatenate([x[j, c] for x in pieces for c in range(2)], axis=0), 0, 1)


def near_kernel(marks, frame_tokens, frames_ref, *refs):
    kvs, (k_out, v_out, bias_out) = refs[:-3], refs[-3:]
    k_out[...] = turn(kvs, 0)
    v_out[...] = turn(kvs, 1)
    clips, length = bias_out.shape
    tokens = length // len(marks)
    me = lax.axis_index("seq")
    key = lax.broadcasted_iota(jnp.int32, (1, length), 1)
    place = jnp.zeros((1, length), jnp.int32)
    for s, mark in enumerate(marks):
        start = jnp.bitwise_xor(me, mark) * tokens - s * tokens
        place = jnp.where(key >= s * tokens, key + start, place)
    for c in range(clips):
        bias_out[c:c + 1, :] = jnp.where(place < frames_ref[c] * frame_tokens, 0.0, neg_large)


def query_kernel(*refs):
    srcs, out = refs[:-1], refs[-1]
    out[...] = turn(srcs, 0)


def attend_kernel(count, q, *refs):
    kvs, (k_near, v_near, bias), outs = refs[:count], refs[count:count + 3], refs[count + 3:]
    k = jnp.concatenate([k_near[...], turn(kvs, 0)], axis=1)
    v = jnp.concatenate([v_near[...], turn(kvs, 1)], axis=1)
    slots = k.shape[0]
    clips = bias.shape[0]
    s = lax.dot_general(q[...], k, (((2,), (2,)), ((0,), (0,))), preferred_element_type=jnp.float32)
    s = s * (1.0 / math.sqrt(HDIM)) + jnp.concatenate([bias[...]] * (slots // clips), axis=0)[:, None, :]
    e = jnp.exp(s - jnp.max(s, axis=2, keepdims=True))
    w = (e / jnp.sum(e, axis=2, keepdims=True)).astype(jnp.bfloat16)
    o = lax.dot_general(w, v, (((2,), (1,)), ((0,), (0,))), preferred_element_type=jnp.float32)
    o = jnp.swapaxes(o.astype(jnp.bfloat16), 0, 1)
    tokens = outs[0].shape[1]
    for i, out in enumerate(outs):
        for c in range(2):
            out[c] = o[(2 * i + c) * tokens:(2 * i + c + 1) * tokens]


def place_kernel(outer, order, *refs):
    kept, came, out = refs[:outer], refs[outer:-1], refs[-1]
    heads = kept[0].shape[2]
    line, core = position(outer)
    for i, a in enumerate(order):
        group = jnp.bitwise_xor(line, a) * 2
        out[:, pl.ds((group + core) * heads, heads)] = kept[i][0]
        out[:, pl.ds((group + 1 - core) * heads, heads)] = came[i][1]


def after(x, y):
    y = y[(0,) * (y.ndim - 1)]
    return jnp.where(y == y, x, jnp.zeros_like(x))


def body(queries, keys, values, clip_frames):
    tokens, clips, features = queries.shape
    devices = lax.axis_size("seq")
    outer = 1
    while outer * outer < devices:
        outer *= 2
    inner = devices // outer
    heads = HEADS // (2 * outer)
    slots = heads * clips
    length = tokens * devices
    bf = jnp.bfloat16

    def swap(x, mask):
        return lax.ppermute(x, "seq", [(i, i ^ mask) for i in range(devices)])

    far = list(range(outer - 1, outer // 2 - 1, -1))
    near = list(range(outer // 2 - 1, -1, -1))
    late = far[len(far) // 2:]
    by_head = [jnp.transpose(x.reshape(tokens, clips, HEADS, HDIM), (0, 2, 1, 3)) for x in (keys, values, queries)]
    kv_peer, kv_own = pack(outer, *by_head[:2])
    q_peer, q_own = pack(outer, by_head[2])
    kv_got, q_got = swap(kv_peer, 1), swap(q_peer, 1)

    kv = {}
    for a in near + far:
        pay = jnp.stack([kv_own[:, a], kv_got[:, a]], axis=1)
        kv[a] = swap(pay, a * inner) if a else pay

    flips = [0]
    step = inner // 2
    while step > 1:
        flips = flips + [m ^ step for m in flips]
        step //= 2

    def across(x):
        pieces = [x]
        step = inner // 2
        while step > 1:
            pieces = pieces + [swap(y, step) for y in pieces]
            step //= 2
        return pieces

    kv[0] = after(kv[0], kv[near[0]])
    crossed = {a: across(kv[a]) for a in near[::-1]}
    every = [(a, n) for a in near[::-1] + far for n in range(len(flips))]
    first = [(a, n) for a, n in every if a == 0 or a in near and n == 0]
    rest = [p for p in every if p not in first]
    marks = [(a * inner) ^ flips[n] ^ c for a, n in first + rest for c in (0, 1)]
    some = jax.ShapeDtypeStruct((slots, 2 * tokens * len(first), HDIM), bf)
    k_near, v_near, bias = pl.pallas_call(
        functools.partial(near_kernel, marks, length // FRAMES),
        out_shape=[some, some, jax.ShapeDtypeStruct((clips, length), jnp.float32)],
        in_specs=[SM] + [VM] * len(first), out_specs=[VM] * 3,
        compiler_params=LARGE, cost_estimate=cost(0.01),
    )(clip_frames, *[crossed[a][n] for a, n in first])

    for a in far:
        if a not in late:
            crossed[a] = across(kv[a])
    parts = far + near
    qs = {}
    for a in parts:
        pay = jnp.stack([q_own[:, a], q_got[:, a]], axis=1)
        qs[a] = swap(after(pay, k_near), a * inner) if a else pay
    for a in late:
        crossed[a] = across(after(kv[a], crossed[near[0]][1]))
    q = pl.pallas_call(
        query_kernel, out_shape=jax.ShapeDtypeStruct((slots, outer * 2 * tokens, HDIM), bf),
        in_specs=[VM] * outer, out_specs=VM, compiler_params=SMALL, cost_estimate=cost(1.3),
    )(*[qs[a] for a in parts])
    piece = jax.ShapeDtypeStruct((2, tokens, slots, HDIM), bf)
    res = pl.pallas_call(
        functools.partial(attend_kernel, len(rest)),
        out_shape=[piece] * outer,
        in_specs=[VM] * (len(rest) + 4), out_specs=[VM] * outer,
        compiler_params=LARGE, cost_estimate=cost(2),
    )(q, *[crossed[a][n] for a, n in rest], k_near, v_near, bias)

    outs = [swap(o, a * inner) if a else o for a, o in zip(parts, res)]
    came = [swap(o, 1) for o in outs]
    out = pl.pallas_call(
        functools.partial(place_kernel, outer, parts),
        out_shape=jax.ShapeDtypeStruct((tokens, HEADS, clips, HDIM), bf),
        in_specs=[VM] * (2 * outer), out_specs=VM, compiler_params=SMALL,
    )(*[x.reshape(2, tokens, heads, clips, HDIM) for x in outs + came])
    return jnp.transpose(out, (0, 2, 1, 3)).reshape(tokens, clips, features)


def solution(mesh):
    return jax.shard_map(
        body,
        mesh=mesh,
        in_specs=(P("seq", "grp", None), P("seq", "grp", None), P("seq", "grp", None), P("grp")),
        out_specs=P("seq", "grp", None),
        check_vma=False,
    )
```

```python
import functools
import math

import jax
import jax.numpy as jnp
from jax import lax
from jax.experimental import pallas as pl
from jax.experimental.pallas import tpu as pltpu
from jax.sharding import PartitionSpec as P

HEADS = 32
HDIM = 128
FRAMES = 8
neg_large = -1e30
VM = pl.BlockSpec(memory_space=pltpu.VMEM)
ANY = pl.BlockSpec(memory_space=pl.ANY)
SM = pl.BlockSpec(memory_space=pltpu.SMEM)
LARGE = pltpu.CompilerParams(vmem_limit_bytes=24 * 1024 * 1024)
SMALL = pltpu.CompilerParams(vmem_limit_bytes=8 * 1024 * 1024)


def cost(micros):
    return pl.CostEstimate(flops=int(micros * 1e9), bytes_accessed=int(micros * 3e6), transcendentals=0)


def position(outer):
    me = lax.axis_index("seq")
    return me // (lax.axis_size("seq") // outer), me % 2


def pack_kernel(outer, count, partners, flip, *refs):
    srcs, dst, sem = refs[:count], refs[count], refs[count + 1]
    heads = dst.shape[3]
    line, core = position(outer)
    copies = []
    for i, a in enumerate(partners):
        group = jnp.bitwise_xor(line, a) * 2 + jnp.bitwise_xor(core, flip)
        for j, src in enumerate(srcs):
            copies.append(pltpu.make_async_copy(
                src.at[:, pl.ds(group * heads, heads)], dst.at[j, i], sem.at[len(copies)]))
    for c in copies:
        c.start()
    for c in copies:
        c.wait()


def pack(outer, partners, flip, params, *srcs):
    tokens, _, clips, _ = srcs[0].shape
    heads = HEADS // (2 * outer)
    out = pl.pallas_call(
        functools.partial(pack_kernel, outer, len(srcs), partners, flip),
        out_shape=jax.ShapeDtypeStruct((len(srcs), len(partners), tokens, heads, clips, HDIM), jnp.bfloat16),
        in_specs=[ANY] * len(srcs), out_specs=VM,
        scratch_shapes=[pltpu.SemaphoreType.DMA((len(partners) * len(srcs),))], compiler_params=params,
    )(*srcs)
    return out.reshape(out.shape[:3] + (heads * clips, HDIM))


def turn(pieces, j):
    return jnp.swapaxes(jnp.concatenate([x[j, c] for x in pieces for c in range(2)], axis=0), 0, 1)


def near_kernel(marks, frame_tokens, frames_ref, *refs):
    kvs, (k_out, v_out, bias_out) = refs[:-3], refs[-3:]
    k_out[...] = turn(kvs, 0)
    v_out[...] = turn(kvs, 1)
    clips, length = bias_out.shape
    tokens = length // len(marks)
    me = lax.axis_index("seq")
    key = lax.broadcasted_iota(jnp.int32, (1, length), 1)
    place = jnp.zeros((1, length), jnp.int32)
    for s, mark in enumerate(marks):
        start = jnp.bitwise_xor(me, mark) * tokens - s * tokens
        place = jnp.where(key >= s * tokens, key + start, place)
    for c in range(clips):
        bias_out[c:c + 1, :] = jnp.where(place < frames_ref[c] * frame_tokens, 0.0, neg_large)


def query_kernel(*refs):
    srcs, out = refs[:-1], refs[-1]
    out[...] = turn(srcs, 0)


def attend_kernel(count, q, *refs):
    kvs, (k_near, v_near, bias), outs = refs[:count], refs[count:count + 3], refs[count + 3:]
    k = jnp.concatenate([k_near[...], turn(kvs, 0)], axis=1)
    v = jnp.concatenate([v_near[...], turn(kvs, 1)], axis=1)
    slots = k.shape[0]
    clips = bias.shape[0]
    s = lax.dot_general(q[...], k, (((2,), (2,)), ((0,), (0,))), preferred_element_type=jnp.float32)
    s = s * (1.0 / math.sqrt(HDIM)) + jnp.concatenate([bias[...]] * (slots // clips), axis=0)[:, None, :]
    e = jnp.exp(s - jnp.max(s, axis=2, keepdims=True))
    w = (e / jnp.sum(e, axis=2, keepdims=True)).astype(jnp.bfloat16)
    o = lax.dot_general(w, v, (((2,), (1,)), ((0,), (0,))), preferred_element_type=jnp.float32)
    o = jnp.swapaxes(o.astype(jnp.bfloat16), 0, 1)
    tokens = outs[0].shape[1]
    for i, out in enumerate(outs):
        for c in range(2):
            out[c] = o[(2 * i + c) * tokens:(2 * i + c + 1) * tokens]


def place_kernel(outer, order, *refs):
    kept, came, out = refs[:outer], refs[outer:-1], refs[-1]
    heads = kept[0].shape[2]
    line, core = position(outer)
    for i, a in enumerate(order):
        group = jnp.bitwise_xor(line, a) * 2
        out[:, pl.ds((group + core) * heads, heads)] = kept[i][0]
        out[:, pl.ds((group + 1 - core) * heads, heads)] = came[i][1]


def after(x, y):
    y = y[(0,) * (y.ndim - 1)]
    return jnp.where(y == y, x, jnp.zeros_like(x))


def body(queries, keys, values, clip_frames):
    tokens, clips, features = queries.shape
    devices = lax.axis_size("seq")
    outer = 1
    while outer * outer < devices:
        outer *= 2
    inner = devices // outer
    heads = HEADS // (2 * outer)
    slots = heads * clips
    length = tokens * devices
    bf = jnp.bfloat16

    def swap(x, mask):
        return lax.ppermute(x, "seq", [(i, i ^ mask) for i in range(devices)])

    far = list(range(outer - 1, outer // 2 - 1, -1))
    near = list(range(outer // 2 - 1, -1, -1))
    late = far[len(far) // 2:]
    by_head = [jnp.transpose(x.reshape(tokens, clips, HEADS, HDIM), (0, 2, 1, 3)) for x in (keys, values, queries)]
    line = list(range(outer))
    soon = near[:-1] + far
    kv_got = {}
    for part, params in ((soon, None), ([a for a in line if a not in soon], SMALL)):
        both = swap(pack(outer, part, 1, params, *by_head[:2]), 1)
        kv_got.update({a: both[:, i] for i, a in enumerate(part)})
    kv_own = pack(outer, line, 0, SMALL, *by_head[:2])
    q_got = swap(pack(outer, line, 1, SMALL, by_head[2]), 1)
    q_own = pack(outer, line, 0, SMALL, by_head[2])

    kv = {}
    for a in far + near:
        pay = jnp.stack([kv_own[:, a], kv_got[a]], axis=1)
        kv[a] = swap(pay, a * inner) if a else pay

    flips = [0]
    step = inner // 2
    while step > 1:
        flips = flips + [m ^ step for m in flips]
        step //= 2

    def across(x):
        pieces = [x]
        step = inner // 2
        while step > 1:
            pieces = pieces + [swap(y, step) for y in pieces]
            step //= 2
        return pieces

    kv[0] = after(kv[0], kv[near[0]])
    crossed = {a: across(kv[a]) for a in near[::-1]}
    every = [(a, n) for a in near[::-1] + far for n in range(len(flips))]
    first = [(a, n) for a, n in every if a == 0 or a in near and n == 0]
    rest = [p for p in every if p not in first]
    marks = [(a * inner) ^ flips[n] ^ c for a, n in first + rest for c in (0, 1)]
    some = jax.ShapeDtypeStruct((slots, 2 * tokens * len(first), HDIM), bf)
    k_near, v_near, bias = pl.pallas_call(
        functools.partial(near_kernel, marks, length // FRAMES),
        out_shape=[some, some, jax.ShapeDtypeStruct((clips, length), jnp.float32)],
        in_specs=[SM] + [VM] * len(first), out_specs=[VM] * 3,
        compiler_params=LARGE, cost_estimate=cost(0.01),
    )(clip_frames, *[crossed[a][n] for a, n in first])

    for a in far:
        if a not in late:
            crossed[a] = across(kv[a])
    parts = far + near
    qs = {}
    for a in parts:
        pay = jnp.stack([q_own[:, a], q_got[:, a]], axis=1)
        qs[a] = swap(after(pay, k_near), a * inner) if a else pay
    for a in late:
        crossed[a] = across(after(kv[a], crossed[near[0]][1]))
    q = pl.pallas_call(
        query_kernel, out_shape=jax.ShapeDtypeStruct((slots, outer * 2 * tokens, HDIM), bf),
        in_specs=[VM] * outer, out_specs=VM, compiler_params=SMALL, cost_estimate=cost(1.3),
    )(*[qs[a] for a in parts])
    piece = jax.ShapeDtypeStruct((2, tokens, slots, HDIM), bf)
    res = pl.pallas_call(
        functools.partial(attend_kernel, len(rest)),
        out_shape=[piece] * outer,
        in_specs=[VM] * (len(rest) + 4), out_specs=[VM] * outer,
        compiler_params=LARGE, cost_estimate=cost(2),
    )(q, *[crossed[a][n] for a, n in rest], k_near, v_near, bias)

    outs = [swap(o, a * inner) if a else o for a, o in zip(parts, res)]
    came = [swap(o, 1) for o in outs]
    out = pl.pallas_call(
        functools.partial(place_kernel, outer, parts),
        out_shape=jax.ShapeDtypeStruct((tokens, HEADS, clips, HDIM), bf),
        in_specs=[VM] * (2 * outer), out_specs=VM, compiler_params=SMALL,
    )(*[x.reshape(2, tokens, heads, clips, HDIM) for x in outs + came])
    return jnp.transpose(out, (0, 2, 1, 3)).reshape(tokens, clips, features)


def solution(mesh):
    return jax.shard_map(
        body,
        mesh=mesh,
        in_specs=(P("seq", "grp", None), P("seq", "grp", None), P("seq", "grp", None), P("grp")),
        out_specs=P("seq", "grp", None),
        check_vma=False,
    )
```

```python
import functools
import math

import jax
import jax.numpy as jnp
from jax import lax
from jax.experimental import pallas as pl
from jax.experimental.pallas import tpu as pltpu
from jax.sharding import PartitionSpec as P

HEADS = 32
HDIM = 128
FRAMES = 8
neg_large = -1e30
VM = pl.BlockSpec(memory_space=pltpu.VMEM)
ANY = pl.BlockSpec(memory_space=pl.ANY)
SM = pl.BlockSpec(memory_space=pltpu.SMEM)
LARGE = pltpu.CompilerParams(vmem_limit_bytes=24 * 1024 * 1024)
SMALL = pltpu.CompilerParams(vmem_limit_bytes=8 * 1024 * 1024)


def cost(micros):
    return pl.CostEstimate(flops=int(micros * 1e9), bytes_accessed=int(micros * 3e6), transcendentals=0)


def position(outer):
    me = lax.axis_index("seq")
    return me // (lax.axis_size("seq") // outer), me % 2


def pack_kernel(outer, count, partners, flip, *refs):
    srcs, dst, sem = refs[:count], refs[count], refs[count + 1]
    heads = dst.shape[3]
    line, core = position(outer)
    copies = []
    for i, a in enumerate(partners):
        group = jnp.bitwise_xor(line, a) * 2 + jnp.bitwise_xor(core, flip)
        for j, src in enumerate(srcs):
            copies.append(pltpu.make_async_copy(
                src.at[:, pl.ds(group * heads, heads)], dst.at[j, i], sem.at[len(copies)]))
    for c in copies:
        c.start()
    for c in copies:
        c.wait()


def pack(outer, partners, flip, params, *srcs):
    tokens, _, clips, _ = srcs[0].shape
    heads = HEADS // (2 * outer)
    out = pl.pallas_call(
        functools.partial(pack_kernel, outer, len(srcs), partners, flip),
        out_shape=jax.ShapeDtypeStruct((len(srcs), len(partners), tokens, heads, clips, HDIM), jnp.bfloat16),
        in_specs=[ANY] * len(srcs), out_specs=VM,
        scratch_shapes=[pltpu.SemaphoreType.DMA((len(partners) * len(srcs),))], compiler_params=params,
    )(*srcs)
    return out.reshape(out.shape[:3] + (heads * clips, HDIM))


def turn(pieces, j):
    return jnp.swapaxes(jnp.concatenate([x[j, c] for x in pieces for c in range(2)], axis=0), 0, 1)


def near_kernel(marks, frame_tokens, frames_ref, *refs):
    kvs, (k_out, v_out, bias_out) = refs[:-3], refs[-3:]
    k_out[...] = turn(kvs, 0)
    v_out[...] = turn(kvs, 1)
    clips, length = bias_out.shape
    tokens = length // len(marks)
    me = lax.axis_index("seq")
    key = lax.broadcasted_iota(jnp.int32, (1, length), 1)
    place = jnp.zeros((1, length), jnp.int32)
    for s, mark in enumerate(marks):
        start = jnp.bitwise_xor(me, mark) * tokens - s * tokens
        place = jnp.where(key >= s * tokens, key + start, place)
    for c in range(clips):
        bias_out[c:c + 1, :] = jnp.where(place < frames_ref[c] * frame_tokens, 0.0, neg_large)


def query_kernel(count, *refs):
    srcs, kvs, (out, k_out, v_out) = refs[:count], refs[count:-3], refs[-3:]
    out[...] = turn(srcs, 0)
    k_out[...] = turn(kvs, 0)
    v_out[...] = turn(kvs, 1)


def attend_kernel(count, q, *refs):
    kvs, (k_near, v_near, k_mid, v_mid, bias), outs = refs[:count], refs[count:count + 5], refs[count + 5:]
    k = jnp.concatenate([k_near[...], k_mid[...], turn(kvs, 0)], axis=1)
    v = jnp.concatenate([v_near[...], v_mid[...], turn(kvs, 1)], axis=1)
    slots = k.shape[0]
    clips = bias.shape[0]
    s = lax.dot_general(q[...], k, (((2,), (2,)), ((0,), (0,))), preferred_element_type=jnp.float32)
    s = s * (1.0 / math.sqrt(HDIM)) + jnp.concatenate([bias[...]] * (slots // clips), axis=0)[:, None, :]
    e = jnp.exp(s - jnp.max(s, axis=2, keepdims=True))
    w = (e * (1.0 / jnp.sum(e, axis=2, keepdims=True))).astype(jnp.bfloat16)
    o = lax.dot_general(w, v, (((2,), (1,)), ((0,), (0,))), preferred_element_type=jnp.float32)
    o = jnp.swapaxes(o.astype(jnp.bfloat16), 0, 1)
    tokens = outs[0].shape[1]
    for i, out in enumerate(outs):
        for c in range(2):
            out[c] = o[(2 * i + c) * tokens:(2 * i + c + 1) * tokens]


def place_kernel(outer, order, *refs):
    kept, came, out = refs[:outer], refs[outer:-1], refs[-1]
    heads = kept[0].shape[2]
    line, core = position(outer)
    for i, a in enumerate(order):
        group = jnp.bitwise_xor(line, a) * 2
        out[:, pl.ds((group + core) * heads, heads)] = kept[i][0]
        out[:, pl.ds((group + 1 - core) * heads, heads)] = came[i][1]


def after(x, y):
    y = y[(0,) * (y.ndim - 1)]
    return jnp.where(y == y, x, jnp.zeros_like(x))


def body(queries, keys, values, clip_frames):
    tokens, clips, features = queries.shape
    devices = lax.axis_size("seq")
    outer = 1
    while outer * outer < devices:
        outer *= 2
    inner = devices // outer
    heads = HEADS // (2 * outer)
    slots = heads * clips
    length = tokens * devices
    bf = jnp.bfloat16

    def swap(x, mask):
        return lax.ppermute(x, "seq", [(i, i ^ mask) for i in range(devices)])

    far = list(range(outer - 1, outer // 2 - 1, -1))
    near = list(range(outer // 2 - 1, -1, -1))
    late = far[len(far) // 2:]
    by_head = [jnp.transpose(x.reshape(tokens, clips, HEADS, HDIM), (0, 2, 1, 3)) for x in (keys, values, queries)]
    line = list(range(outer))
    soon = near[:-1] + far
    kv_got = {}
    for part, params in ((soon, None), ([a for a in line if a not in soon], SMALL)):
        both = swap(pack(outer, part, 1, params, *by_head[:2]), 1)
        kv_got.update({a: both[:, i] for i, a in enumerate(part)})
    kv_own = pack(outer, line, 0, SMALL, *by_head[:2])
    q_got = swap(pack(outer, line, 1, SMALL, by_head[2]), 1)
    q_own = pack(outer, line, 0, SMALL, by_head[2])

    kv = {}
    for a in far + near:
        pay = jnp.stack([kv_own[:, a], kv_got[a]], axis=1)
        kv[a] = swap(pay, a * inner) if a else pay

    flips = [0]
    step = inner // 2
    while step > 1:
        flips = flips + [m ^ step for m in flips]
        step //= 2

    def across(x):
        pieces = [x]
        step = inner // 2
        while step > 1:
            pieces = pieces + [swap(y, step) for y in pieces]
            step //= 2
        return pieces

    kv[0] = after(kv[0], kv[near[0]])
    crossed = {a: across(kv[a]) for a in near[::-1]}
    every = [(a, n) for a in near[::-1] + far for n in range(len(flips))]
    first = [(a, n) for a, n in every if a == 0 or a in near and n == 0]
    last = [(a, n) for a, n in every if a in late and n]
    middle = [p for p in every if p not in first and p not in last]
    rest = middle + last
    marks = [(a * inner) ^ flips[n] ^ c for a, n in first + rest for c in (0, 1)]
    some = jax.ShapeDtypeStruct((slots, 2 * tokens * len(first), HDIM), bf)
    k_near, v_near, bias = pl.pallas_call(
        functools.partial(near_kernel, marks, length // FRAMES),
        out_shape=[some, some, jax.ShapeDtypeStruct((clips, length), jnp.float32)],
        in_specs=[SM] + [VM] * len(first), out_specs=[VM] * 3,
        compiler_params=LARGE, cost_estimate=cost(0.01),
    )(clip_frames, *[crossed[a][n] for a, n in first])

    for a in far:
        if a not in late:
            crossed[a] = across(kv[a])
    parts = far + near
    qs = {}
    for a in parts:
        pay = jnp.stack([q_own[:, a], q_got[:, a]], axis=1)
        qs[a] = swap(after(pay, k_near), a * inner) if a else pay
    for a in late:
        crossed[a] = across(after(kv[a], crossed[near[0]][1]))
    most = jax.ShapeDtypeStruct((slots, 2 * tokens * len(middle), HDIM), bf)
    q, k_mid, v_mid = pl.pallas_call(
        functools.partial(query_kernel, outer),
        out_shape=[jax.ShapeDtypeStruct((slots, outer * 2 * tokens, HDIM), bf), most, most],
        in_specs=[VM] * (outer + len(middle)), out_specs=[VM] * 3, compiler_params=LARGE, cost_estimate=cost(1.3),
    )(*[qs[a] for a in parts], *[crossed[a][n] for a, n in middle])
    piece = jax.ShapeDtypeStruct((2, tokens, slots, HDIM), bf)
    res = pl.pallas_call(
        functools.partial(attend_kernel, len(last)),
        out_shape=[piece] * outer,
        in_specs=[VM] * (len(last) + 6), out_specs=[VM] * outer,
        compiler_params=LARGE, cost_estimate=cost(2),
    )(q, *[crossed[a][n] for a, n in last], k_near, v_near, k_mid, v_mid, bias)

    outs = [swap(o, a * inner) if a else o for a, o in zip(parts, res)]
    came = [swap(o, 1) for o in outs]
    out = pl.pallas_call(
        functools.partial(place_kernel, outer, parts),
        out_shape=jax.ShapeDtypeStruct((tokens, HEADS, clips, HDIM), bf),
        in_specs=[VM] * (2 * outer), out_specs=VM, compiler_params=SMALL,
    )(*[x.reshape(2, tokens, heads, clips, HDIM) for x in outs + came])
    return jnp.transpose(out, (0, 2, 1, 3)).reshape(tokens, clips, features)


def solution(mesh):
    return jax.shard_map(
        body,
        mesh=mesh,
        in_specs=(P("seq", "grp", None), P("seq", "grp", None), P("seq", "grp", None), P("grp")),
        out_specs=P("seq", "grp", None),
        check_vma=False,
    )
```

```python
import functools
import math

import jax
import jax.numpy as jnp
from jax import lax
from jax.experimental import pallas as pl
from jax.experimental.pallas import tpu as pltpu
from jax.sharding import PartitionSpec as P

HEADS = 32
HDIM = 128
FRAMES = 8
neg_large = -1e30
VM = pl.BlockSpec(memory_space=pltpu.VMEM)
ANY = pl.BlockSpec(memory_space=pl.ANY)
SM = pl.BlockSpec(memory_space=pltpu.SMEM)
LARGE = pltpu.CompilerParams(vmem_limit_bytes=24 * 1024 * 1024)
SMALL = pltpu.CompilerParams(vmem_limit_bytes=8 * 1024 * 1024)


def cost(micros):
    return pl.CostEstimate(flops=int(micros * 1e9), bytes_accessed=int(micros * 3e6), transcendentals=0)


def position(outer):
    me = lax.axis_index("seq")
    return me // (lax.axis_size("seq") // outer), me % 2


def pack_kernel(outer, count, partners, flip, *refs):
    srcs, dst, sem = refs[:count], refs[count], refs[count + 1]
    heads = dst.shape[3]
    line, core = position(outer)
    copies = []
    for i, a in enumerate(partners):
        group = jnp.bitwise_xor(line, a) * 2 + jnp.bitwise_xor(core, flip)
        for j, src in enumerate(srcs):
            copies.append(pltpu.make_async_copy(
                src.at[:, pl.ds(group * heads, heads)], dst.at[j, i], sem.at[len(copies)]))
    for c in copies:
        c.start()
    for c in copies:
        c.wait()


def pack(outer, partners, flip, params, *srcs):
    tokens, _, clips, _ = srcs[0].shape
    heads = HEADS // (2 * outer)
    out = pl.pallas_call(
        functools.partial(pack_kernel, outer, len(srcs), partners, flip),
        out_shape=jax.ShapeDtypeStruct((len(srcs), len(partners), tokens, heads, clips, HDIM), jnp.bfloat16),
        in_specs=[ANY] * len(srcs), out_specs=VM,
        scratch_shapes=[pltpu.SemaphoreType.DMA((len(partners) * len(srcs),))], compiler_params=params,
    )(*srcs)
    return out.reshape(out.shape[:3] + (heads * clips, HDIM))


def turn(pieces, j):
    return jnp.swapaxes(jnp.concatenate([x[j, c] for x in pieces for c in range(2)], axis=0), 0, 1)


def near_kernel(marks, frame_tokens, frames_ref, *refs):
    kvs, (k_out, v_out, bias_out) = refs[:-3], refs[-3:]
    k_out[...] = turn(kvs, 0)
    v_out[...] = turn(kvs, 1)
    clips, length = bias_out.shape
    tokens = length // len(marks)
    me = lax.axis_index("seq")
    key = lax.broadcasted_iota(jnp.int32, (1, length), 1)
    place = jnp.zeros((1, length), jnp.int32)
    for s, mark in enumerate(marks):
        start = jnp.bitwise_xor(me, mark) * tokens - s * tokens
        place = jnp.where(key >= s * tokens, key + start, place)
    for c in range(clips):
        bias_out[c:c + 1, :] = jnp.where(place < frames_ref[c] * frame_tokens, 0.0, neg_large)


def query_kernel(*refs):
    srcs, out = refs[:-1], refs[-1]
    out[...] = turn(srcs, 0)


def attend_kernel(count, q, *refs):
    kvs, (k_near, v_near, bias), outs = refs[:count], refs[count:count + 3], refs[count + 3:]
    k = jnp.concatenate([k_near[...], turn(kvs, 0)], axis=1)
    v = jnp.concatenate([v_near[...], turn(kvs, 1)], axis=1)
    slots = k.shape[0]
    clips = bias.shape[0]
    s = lax.dot_general(q[...], k, (((2,), (2,)), ((0,), (0,))), preferred_element_type=jnp.float32)
    s = s * (1.0 / math.sqrt(HDIM)) + jnp.concatenate([bias[...]] * (slots // clips), axis=0)[:, None, :]
    e = jnp.exp(s - jnp.max(s, axis=2, keepdims=True))
    w = (e * (1.0 / jnp.sum(e, axis=2, keepdims=True))).astype(jnp.bfloat16)
    o = lax.dot_general(w, v, (((2,), (1,)), ((0,), (0,))), preferred_element_type=jnp.float32)
    o = jnp.swapaxes(o.astype(jnp.bfloat16), 0, 1)
    tokens = outs[0].shape[1]
    for i, out in enumerate(outs):
        for c in range(2):
            out[c] = o[(2 * i + c) * tokens:(2 * i + c + 1) * tokens]


def place_kernel(outer, order, *refs):
    kept, came, out = refs[:outer], refs[outer:-1], refs[-1]
    heads = kept[0].shape[2]
    line, core = position(outer)
    for i, a in enumerate(order):
        group = jnp.bitwise_xor(line, a) * 2
        out[:, pl.ds((group + core) * heads, heads)] = kept[i][0]
        out[:, pl.ds((group + 1 - core) * heads, heads)] = came[i][1]


def after(x, y):
    y = y[(0,) * (y.ndim - 1)]
    return jnp.where(y == y, x, jnp.zeros_like(x))


def body(queries, keys, values, clip_frames):
    tokens, clips, features = queries.shape
    devices = lax.axis_size("seq")
    outer = 1
    while outer * outer < devices:
        outer *= 2
    inner = devices // outer
    heads = HEADS // (2 * outer)
    slots = heads * clips
    length = tokens * devices
    bf = jnp.bfloat16

    def swap(x, mask):
        return lax.ppermute(x, "seq", [(i, i ^ mask) for i in range(devices)])

    far = list(range(outer - 1, outer // 2 - 1, -1))
    near = list(range(outer // 2 - 1, -1, -1))
    late = far[len(far) // 2:]
    by_head = [jnp.transpose(x.reshape(tokens, clips, HEADS, HDIM), (0, 2, 1, 3)) for x in (keys, values, queries)]
    line = list(range(outer))
    soon = near[:-1] + far
    kv_got = {}
    for part, params in ((soon, None), ([a for a in line if a not in soon], SMALL)):
        both = swap(pack(outer, part, 1, params, *by_head[:2]), 1)
        kv_got.update({a: both[:, i] for i, a in enumerate(part)})
    kv_own = pack(outer, line, 0, SMALL, *by_head[:2])
    q_got = swap(pack(outer, line, 1, SMALL, by_head[2]), 1)
    q_own = pack(outer, line, 0, SMALL, by_head[2])

    kv = {}
    for a in far + near:
        pay = jnp.stack([kv_own[:, a], kv_got[a]], axis=1)
        kv[a] = swap(pay, a * inner) if a else pay

    flips = [0]
    step = inner // 2
    while step > 1:
        flips = flips + [m ^ step for m in flips]
        step //= 2

    def across(x):
        pieces = [x]
        step = inner // 2
        while step > 1:
            pieces = pieces + [swap(y, step) for y in pieces]
            step //= 2
        return pieces

    kv[0] = after(kv[0], kv[near[0]])
    crossed = {a: across(kv[a]) for a in near[::-1]}
    every = [(a, n) for a in near[::-1] + far for n in range(len(flips))]
    first = [(a, n) for a, n in every if a == 0 or a in near and n == 0]
    rest = [p for p in every if p not in first]
    marks = [(a * inner) ^ flips[n] ^ c for a, n in first + rest for c in (0, 1)]
    some = jax.ShapeDtypeStruct((slots, 2 * tokens * len(first), HDIM), bf)
    k_near, v_near, bias = pl.pallas_call(
        functools.partial(near_kernel, marks, length // FRAMES),
        out_shape=[some, some, jax.ShapeDtypeStruct((clips, length), jnp.float32)],
        in_specs=[SM] + [VM] * len(first), out_specs=[VM] * 3,
        compiler_params=LARGE, cost_estimate=cost(0.01),
    )(clip_frames, *[crossed[a][n] for a, n in first])

    for a in far:
        if a not in late:
            crossed[a] = across(kv[a])
    parts = far + near
    qs = {}
    for a in parts:
        pay = jnp.stack([q_own[:, a], q_got[:, a]], axis=1)
        qs[a] = swap(after(pay, k_near), a * inner) if a else pay
    for a in late:
        crossed[a] = across(after(kv[a], crossed[near[0]][1]))
    q = pl.pallas_call(
        query_kernel, out_shape=jax.ShapeDtypeStruct((slots, outer * 2 * tokens, HDIM), bf),
        in_specs=[VM] * outer, out_specs=VM, compiler_params=SMALL, cost_estimate=cost(0.9),
    )(*[qs[a] for a in parts])
    piece = jax.ShapeDtypeStruct((2, tokens, slots, HDIM), bf)
    res = pl.pallas_call(
        functools.partial(attend_kernel, len(rest)),
        out_shape=[piece] * outer,
        in_specs=[VM] * (len(rest) + 4), out_specs=[VM] * outer,
        compiler_params=LARGE, cost_estimate=cost(2),
    )(q, *[crossed[a][n] for a, n in rest], k_near, v_near, bias)

    outs = [swap(o, a * inner) if a else o for a, o in zip(parts, res)]
    came = [swap(o, 1) for o in outs]
    out = pl.pallas_call(
        functools.partial(place_kernel, outer, parts),
        out_shape=jax.ShapeDtypeStruct((tokens, HEADS, clips, HDIM), bf),
        in_specs=[VM] * (2 * outer), out_specs=VM, compiler_params=SMALL,
    )(*[x.reshape(2, tokens, heads, clips, HDIM) for x in outs + came])
    return jnp.transpose(out, (0, 2, 1, 3)).reshape(tokens, clips, features)


def solution(mesh):
    return jax.shard_map(
        body,
        mesh=mesh,
        in_specs=(P("seq", "grp", None), P("seq", "grp", None), P("seq", "grp", None), P("grp")),
        out_specs=P("seq", "grp", None),
        check_vma=False,
    )
```
